32 devices in a mesh: grp: 2 (over y), row: 4 (over z), aux: 2 (over x), col: 2 (over core).
Axes of the slice: x: 2, y: 2, z: 4, core: 2. Of those that a mesh axis runs over, the one named last changes fastest.
Arguments:
- aux_slab: bfloat16 [16, 4096, 4096], P(('grp', 'aux'), 'row', 'col'), parts along dimension 0, may hold values from -6 to 6
- occupied: bfloat16 [4096, 256], P('col', 'grp'), parts along dimension 1, may hold values from -0.01171875 to 0.01171875
Outputs:
- exchange: float32 [8192, 4096], P(('grp', 'aux', 'col'), 'row'), parts along dimension 0
The draws below stay inside these ranges and needn't reach their ends.
There are 2 independent parts, one for each index of `grp`. The reference program is written for one: setup_inputs(seed, part) draws one part's arguments, and reference() takes and returns one part's arrays. A program takes and returns all parts, laid end to end along the dimension named above; each array names one. Nothing has to cross between parts.
All inputs are finite; a program needn't handle non-finite values.
Results may differ from the reference program's by a relative error of at most 0.015.
Values may be sent and summed in bfloat16 or wider, within the bound.
A program may use at most 128 MiB of HBM per device.

```python
import jax
import jax.numpy as jnp
from jax import lax

NBF = 4096
NOCC = 128
AUX_DEV = 4
NAUX = 8
N_AUX = 2
N_COL = 2


def block_levels(key, shape, split, least, high):
    factor_of, own = 1.0, jax.random.fold_in(key, 6)
    for axis_at, blocks in split:
        draws = jnp.exp(jax.random.uniform(jax.random.fold_in(own, axis_at), (blocks,), jnp.float32, least / len(split), high / len(split)))
        factor_of = factor_of * jnp.repeat(draws, shape[axis_at] // blocks).reshape([-1 if axis == axis_at else 1 for axis in range(len(shape))])
    return factor_of


def centred(key, shape, scale, reach, pieces=(), held_as=jnp.bfloat16):
    gain = block_levels(key, shape, pieces, -0.22, 0.18) if pieces else 1.0
    values = jax.random.normal(key, shape, jnp.float32) * scale * gain
    return jnp.minimum(jnp.maximum(values, -reach), reach).astype(held_as)


def setup_inputs(seed: int = 0, part: int = 0) -> dict:
    key_of = jax.random.split(jax.random.key(seed), 3)
    part_splits = jax.random.split(jax.random.fold_in(key_of[2], part), 3)
    return {
        "aux_slab": centred(part_splits[0], (NAUX, NBF, NBF), 1.0, 6.0, ((0, 2), (1, 4), (2, 2))),
        "occupied": centred(part_splits[1], (NBF, NOCC), (64 * NBF) ** -0.5, 0.01171875, ((0, 2),)),
    }


def reference(aux_slab, occupied):
    def transform(slab_plane):
        return jnp.dot(slab_plane, occupied, preferred_element_type=jnp.float32)

    mixed = lax.map(transform, aux_slab)
    panel = mixed.astype(jnp.bfloat16)
    half_width = NOCC // N_COL
    panel = panel.reshape(N_AUX, AUX_DEV, NBF, N_COL, half_width)
    groups = jnp.transpose(panel, (0, 3, 2, 1, 4)).reshape(N_AUX * N_COL, NBF, AUX_DEV * half_width)

    def accumulate(total, block):
        coarse = jnp.dot(block, block.T, preferred_element_type=jnp.float32).astype(jnp.bfloat16)
        coarse = lax.optimization_barrier(coarse)
        return total + coarse.astype(jnp.float32), None

    exchange, _ = lax.scan(accumulate, jnp.zeros((NBF, NBF), jnp.float32), groups)
    return exchange
```

```python
import functools

import jax
import jax.numpy as jnp
from jax import lax
from jax.experimental import pallas as pl
from jax.experimental.pallas import tpu as pltpu
from jax.sharding import PartitionSpec as P

MESH = pl.DeviceIdType.MESH
LAG = 2


def kernel(sizes, slab_hbm, occ_ref, out_ref, slab, pown, psend, precv, held, left_op, right_op, stage,
           s_slab, s_ps, r_ps, s_up, s_down, r_held, s_a, r_a, s_bx, s_bc, s_bf, r_b, s_out):
    nr, na, nc, chunks, rows, depth, occ = sizes
    planes = na * nc
    share = depth // nc
    z, x, s = lax.axis_index("row"), lax.axis_index("aux"), lax.axis_index("col")
    other = 1 - s
    q = x * nc + s
    dist = jnp.abs(z - q)

    def slab_copy(c):
        return pltpu.make_async_copy(
            slab_hbm.at[:, pl.ds(pl.multiple_of(c * rows, rows), rows), :], slab.at[c], s_slab.at[c])

    def remote(src, dst, send, recv, device):
        return pltpu.make_async_remote_copy(
            src_ref=src, dst_ref=dst, send_sem=send, recv_sem=recv, device_id=device, device_id_type=MESH)

    def to_partner(c):
        return remote(psend.at[c], precv.at[c], s_ps.at[c], r_ps.at[c], {"col": other})

    def up(r, c):
        return remote(held.at[r, c], held.at[r, c], s_up.at[r, c], r_held.at[r, c], {"row": lax.rem(z + 1, nr)})

    def down(r, c):
        return remote(held.at[r, c], held.at[r, c], s_down.at[r, c], r_held.at[r, c], {"row": lax.rem(z + nr - 1, nr)})

    def to_owner(r, c):
        return remote(held.at[r, c], left_op.at[q, c], s_a.at[r, c], r_a.at[q, c],
                      {"aux": r // nc, "col": lax.rem(r, nc)})

    def own_across(j, c):
        return remote(held.at[z, c], right_op.at[q, c], s_bx.at[j - 1, c], r_b.at[q, c], {"aux": lax.rem(x + j, na)})

    def own_beside(c):
        return remote(held.at[z, c], right_op.at[q, c], s_bc.at[c], r_b.at[q, c], {"col": other})

    def pass_beside(j, c):
        qq = lax.rem(x + j, na) * nc + s
        return remote(right_op.at[qq, c], right_op.at[qq, c], s_bf.at[j - 1, c], r_b.at[qq, c], {"col": other})

    def b_wait(qq, c):
        remote(right_op.at[qq, c], right_op.at[qq, c], s_bc.at[c], r_b.at[qq, c], {"col": other}).wait_recv()

    def a_wait(qq, c):
        remote(left_op.at[qq, c], left_op.at[qq, c], s_bc.at[c], r_a.at[qq, c], {"col": other}).wait_recv()

    def out_copy(c):
        return pltpu.make_async_copy(
            stage.at[c], out_ref.at[pl.ds(pl.multiple_of(c * rows, rows), rows), :], s_out.at[c])

    @pl.loop(0, chunks)
    def _(c):
        slab_copy(c).start()

    barrier = pltpu.get_barrier_semaphore()

    @pl.when(z > 0)
    def _():
        pl.semaphore_signal(barrier, inc=1, device_id={"row": lax.rem(z + nr - 1, nr)}, device_id_type=MESH)

    @pl.when(z < nr - 1)
    def _():
        pl.semaphore_signal(barrier, inc=1, device_id={"row": lax.rem(z + 1, nr)}, device_id_type=MESH)

    for j in range(1, planes):
        peer = lax.rem(q + j, planes)
        pl.semaphore_signal(barrier, inc=1, device_id={"aux": peer // nc, "col": lax.rem(peer, nc)}, device_id_type=MESH)
    ends = (z == 0).astype(jnp.int32) + (z == nr - 1).astype(jnp.int32)
    pl.semaphore_wait(barrier, planes + 1 - ends)

    def partial(c, side):
        block = slab[c, pl.ds(side * share, share)].reshape(share * rows, slab.shape[-1])
        return jnp.dot(block, occ_ref[...], preferred_element_type=jnp.float32)

    def finish(c):
        to_partner(c).wait_recv()
        own = (pown[c] + precv[c].astype(jnp.float32)).astype(held.dtype)
        held[z, c] = own

        @pl.when(z < nr - 1)
        def _():
            up(z, c).start()

        @pl.when(z > 0)
        def _():
            down(z, c).start()

        for j in range(1, na):
            own_across(j, c).start()
        own_beside(c).start()
        right_op[q, c] = own

    @pl.loop(0, chunks)
    def _(c):
        slab_copy(c).wait()
        given = partial(c, other).astype(psend.dtype)
        for k in range(share):
            psend[c, :, k * occ:(k + 1) * occ] = given[k * rows:(k + 1) * rows]
        to_partner(c).start()
        kept = partial(c, s)
        for k in range(share):
            pown[c, :, k * occ:(k + 1) * occ] = kept[k * rows:(k + 1) * rows]

        @pl.when(c > 0)
        def _():
            finish(c - 1)

    finish(chunks - 1)

    def hand_over(r, c):
        @pl.when(r != q)
        def _():
            to_owner(r, c).start()

        @pl.when(r == q)
        def _():
            left_op[q, c] = held[r, c]

    def product(k):
        @pl.when(dist > 0)
        def _():
            for j in range(1, planes):
                a_wait(lax.rem(q + j, planes), k)

        total = None
        for p in range(planes):
            term = lax.dot_general(
                left_op[p, k], right_op[p].reshape(chunks * rows, share * occ),
                (((1,), (1,)), ((), ())), preferred_element_type=jnp.float32)
            total = term if total is None else total + term
        stage[k] = total
        out_copy(k).start()

    first = (jnp.maximum(dist, 2) - 1) * chunks + LAG
    steps = (nr - 1) * chunks

    @pl.loop(0, max(nr - 1, 2) * chunks + LAG)
    def _(t):
        d = t // chunks + 1
        c = lax.rem(t, chunks)

        @pl.when((t < steps) & (z - d >= 0))
        def _():
            r = z - d
            up(r, c).wait_recv()

            @pl.when(z < nr - 1)
            def _():
                up(r, c).start()

            hand_over(r, c)

        @pl.when((t < steps) & (z + d < nr))
        def _():
            r = z + d
            down(r, c).wait_recv()

            @pl.when(z > 0)
            def _():
                down(r, c).start()

            hand_over(r, c)

        @pl.when(t < chunks)
        def _():
            for j in range(1, na):
                b_wait(lax.rem(x + j, na) * nc + s, c)
                pass_beside(j, c).start()

        @pl.when(t == first)
        def _():
            for j in range(na):
                @pl.loop(0, chunks)
                def _(e):
                    b_wait(lax.rem(x + j, na) * nc + other, e)

        @pl.when((t == first) & (dist == 0))
        def _():
            for p in range(planes):
                @pl.loop(0, chunks)
                def _(e):
                    left_op[p, e] = right_op[p, e]

        @pl.when((t >= first) & (t < first + chunks))
        def _():
            product(t - first)

    @pl.loop(0, chunks)
    def _(c):
        to_partner(c).wait_send()
        own_beside(c).wait_send()
        for j in range(1, na):
            own_across(j, c).wait_send()
            pass_beside(j, c).wait_send()

        @pl.loop(0, nr)
        def _(r):
            @pl.when((r <= z) & (z < nr - 1))
            def _():
                up(r, c).wait_send()

            @pl.when((r >= z) & (z > 0))
            def _():
                down(r, c).wait_send()

            @pl.when((r != z) & (r != q))
            def _():
                to_owner(r, c).wait_send()

        out_copy(c).wait()


def body(sizes, slab, occupied):
    nr, na, nc, chunks, rows, depth, occ = sizes
    planes, width = na * nc, depth // nc * occ
    block = chunks * rows
    any_space = pl.BlockSpec(memory_space=pl.ANY)
    dma = pltpu.SemaphoreType.DMA
    bf16 = jnp.bfloat16
    return pl.pallas_call(
        functools.partial(kernel, sizes),
        out_shape=jax.ShapeDtypeStruct((block, block), jnp.float32),
        in_specs=[any_space, pl.BlockSpec(memory_space=pltpu.VMEM)],
        out_specs=any_space,
        scratch_shapes=[
            pltpu.VMEM((chunks, depth, rows, slab.shape[2]), bf16),
            pltpu.VMEM((chunks, rows, width), jnp.float32),
            pltpu.VMEM((chunks, rows, width), bf16),
            pltpu.VMEM((chunks, rows, width), bf16),
            pltpu.VMEM((nr, chunks, rows, width), bf16),
            pltpu.VMEM((planes, chunks, rows, width), bf16),
            pltpu.VMEM((planes, chunks, rows, width), bf16),
            pltpu.VMEM((chunks, rows, block), jnp.float32),
            dma((chunks,)), dma((chunks,)), dma((chunks,)),
            dma((nr, chunks)), dma((nr, chunks)), dma((nr, chunks)),
            dma((nr, chunks)), dma((planes, chunks)),
            dma((na - 1, chunks)), dma((chunks,)), dma((na - 1, chunks)), dma((planes, chunks)),
            dma((chunks,)),
        ],
        compiler_params=pltpu.CompilerParams(
            collective_id=0, has_side_effects=True, vmem_limit_bytes=48 * 2**20),
    )(slab, occupied)


def solution(mesh):
    nr, na, nc = mesh.shape["row"], mesh.shape["aux"], mesh.shape["col"]
    if nc != 2 or na * nc != nr:
        raise ValueError("unsupported mesh")
    ng = mesh.shape["grp"]

    def run(aux_slab, occupied):
        depth = aux_slab.shape[0] // (ng * na)
        block = aux_slab.shape[1] // nr
        rows = min(128, block)
        sizes = (nr, na, nc, block // rows, rows, depth, occupied.shape[1] // ng)
        in_specs = (P(("grp", "aux"), "row", "col"), P("col", "grp"))
        out_specs = P(("grp", "aux", "col"), "row")
        return jax.shard_map(
            functools.partial(body, sizes), mesh=mesh, in_specs=in_specs, out_specs=out_specs, check_vma=False,
        )(aux_slab, occupied)

    return run
```

```python
import functools

import jax
import jax.numpy as jnp
from jax import lax
from jax.experimental import pallas as pl
from jax.experimental.pallas import tpu as pltpu
from jax.sharding import PartitionSpec as P

MESH = pl.DeviceIdType.MESH
LAG = 2


def kernel(sizes, slab_hbm, occ_hbm, out_ref, occ_ref, slab, pown, psend, precv, held, left_op, right_op, stage,
           s_slab, s_ps, r_ps, s_up, s_down, r_held, s_a, r_a, s_bx, s_bc, s_bf, r_b, s_out, s_occ):
    nr, na, nc, chunks, rows, depth, occ = sizes
    planes = na * nc
    share = depth // nc
    z, x, s = lax.axis_index("row"), lax.axis_index("aux"), lax.axis_index("col")
    other = 1 - s
    q = x * nc + s
    dist = jnp.abs(z - q)

    def slab_copy(c):
        return pltpu.make_async_copy(
            slab_hbm.at[:, pl.ds(pl.multiple_of(c * rows, rows), rows), :], slab.at[c], s_slab.at[c])

    def remote(src, dst, send, recv, device):
        return pltpu.make_async_remote_copy(
            src_ref=src, dst_ref=dst, send_sem=send, recv_sem=recv, device_id=device, device_id_type=MESH)

    def to_partner(c):
        return remote(psend.at[c], precv.at[c], s_ps.at[c], r_ps.at[c], {"col": other})

    def up(r, c):
        return remote(held.at[r, c], held.at[r, c], s_up.at[r, c], r_held.at[r, c], {"row": lax.rem(z + 1, nr)})

    def down(r, c):
        return remote(held.at[r, c], held.at[r, c], s_down.at[r, c], r_held.at[r, c], {"row": lax.rem(z + nr - 1, nr)})

    def to_owner(r, c):
        return remote(held.at[r, c], left_op.at[q, c], s_a.at[r, c], r_a.at[q, c],
                      {"aux": r // nc, "col": lax.rem(r, nc)})

    def own_across(j, c):
        return remote(held.at[z, c], right_op.at[q, c], s_bx.at[j - 1, c], r_b.at[q, c], {"aux": lax.rem(x + j, na)})

    def own_beside(c):
        return remote(held.at[z, c], right_op.at[q, c], s_bc.at[c], r_b.at[q, c], {"col": other})

    def pass_beside(j, c):
        qq = lax.rem(x + j, na) * nc + s
        return remote(right_op.at[qq, c], right_op.at[qq, c], s_bf.at[j - 1, c], r_b.at[qq, c], {"col": other})

    def b_wait(qq, c):
        remote(right_op.at[qq, c], right_op.at[qq, c], s_bc.at[c], r_b.at[qq, c], {"col": other}).wait_recv()

    def a_wait(qq, c):
        remote(left_op.at[qq, c], left_op.at[qq, c], s_bc.at[c], r_a.at[qq, c], {"col": other}).wait_recv()

    def out_copy(c):
        return pltpu.make_async_copy(
            stage.at[c], out_ref.at[pl.ds(pl.multiple_of(c * rows, rows), rows), :], s_out.at[c])

    slab_copy(0).start()
    occ_copy = pltpu.make_async_copy(occ_hbm, occ_ref, s_occ)
    occ_copy.start()

    @pl.loop(1, min(2, chunks))
    def _(c):
        slab_copy(c).start()

    barrier = pltpu.get_barrier_semaphore()

    @pl.when(z > 0)
    def _():
        pl.semaphore_signal(barrier, inc=1, device_id={"row": lax.rem(z + nr - 1, nr)}, device_id_type=MESH)

    @pl.when(z < nr - 1)
    def _():
        pl.semaphore_signal(barrier, inc=1, device_id={"row": lax.rem(z + 1, nr)}, device_id_type=MESH)

    for j in range(1, planes):
        peer = lax.rem(q + j, planes)
        pl.semaphore_signal(barrier, inc=1, device_id={"aux": peer // nc, "col": lax.rem(peer, nc)}, device_id_type=MESH)
    ends = (z == 0).astype(jnp.int32) + (z == nr - 1).astype(jnp.int32)
    pl.semaphore_wait(barrier, planes + 1 - ends)

    occ_copy.wait()

    def partial(c, side):
        block = slab[c, pl.ds(side * share, share)].reshape(share * rows, slab.shape[-1])
        return jnp.dot(block, occ_ref[...], preferred_element_type=jnp.float32)

    def finish(c):
        to_partner(c).wait_recv()
        own = (pown[c] + precv[c].astype(jnp.float32)).astype(held.dtype)
        held[z, c] = own

        @pl.when(z < nr - 1)
        def _():
            up(z, c).start()

        @pl.when(z > 0)
        def _():
            down(z, c).start()

        for j in range(1, na):
            own_across(j, c).start()
        own_beside(c).start()
        right_op[q, c] = own

    @pl.loop(0, chunks)
    def _(c):
        slab_copy(c).wait()

        @pl.when(c + 2 < chunks)
        def _():
            slab_copy(c + 2).start()

        given = partial(c, other).astype(psend.dtype)
        for k in range(share):
            psend[c, :, k * occ:(k + 1) * occ] = given[k * rows:(k + 1) * rows]
        to_partner(c).start()

        @pl.when(c > 0)
        def _():
            finish(c - 1)

        kept = partial(c, s)
        for k in range(share):
            pown[c, :, k * occ:(k + 1) * occ] = kept[k * rows:(k + 1) * rows]

    finish(chunks - 1)

    def hand_over(r, c):
        @pl.when(r != q)
        def _():
            to_owner(r, c).start()

        @pl.when(r == q)
        def _():
            left_op[q, c] = held[r, c]

    def product(k):
        @pl.when(dist > 0)
        def _():
            for j in range(1, planes):
                a_wait(lax.rem(q + j, planes), k)

        total = None
        for p in range(planes):
            term = lax.dot_general(
                left_op[p, k], right_op[p].reshape(chunks * rows, share * occ),
                (((1,), (1,)), ((), ())), preferred_element_type=jnp.float32)
            total = term if total is None else total + term
        stage[k] = total
        out_copy(k).start()

    relays = (z > 0) & (z < nr - 1)
    first = jnp.where(relays, max(nr - 2, 1), jnp.maximum(dist, 2) - 1) * chunks + LAG
    steps = (nr - 1) * chunks

    @pl.loop(0, max(nr - 1, 2) * chunks + LAG)
    def _(t):
        d = t // chunks + 1
        c = lax.rem(t, chunks)

        @pl.when((t < steps) & (z - d >= 0))
        def _():
            r = z - d
            up(r, c).wait_recv()

            @pl.when(z < nr - 1)
            def _():
                up(r, c).start()

            hand_over(r, c)

        @pl.when((t < steps) & (z + d < nr))
        def _():
            r = z + d
            down(r, c).wait_recv()

            @pl.when(z > 0)
            def _():
                down(r, c).start()

            hand_over(r, c)

        @pl.when(t < chunks)
        def _():
            for j in range(1, na):
                b_wait(lax.rem(x + j, na) * nc + s, c)
                pass_beside(j, c).start()

        @pl.when(t == first)
        def _():
            for j in range(na):
                @pl.loop(0, chunks)
                def _(e):
                    b_wait(lax.rem(x + j, na) * nc + other, e)

        @pl.when((t == first) & (dist == 0))
        def _():
            for p in range(planes):
                @pl.loop(0, chunks)
                def _(e):
                    left_op[p, e] = right_op[p, e]

        @pl.when((t >= first) & (t < first + chunks))
        def _():
            product(t - first)

    @pl.loop(0, chunks)
    def _(c):
        to_partner(c).wait_send()
        own_beside(c).wait_send()
        for j in range(1, na):
            own_across(j, c).wait_send()
            pass_beside(j, c).wait_send()

        @pl.loop(0, nr)
        def _(r):
            @pl.when((r <= z) & (z < nr - 1))
            def _():
                up(r, c).wait_send()

            @pl.when((r >= z) & (z > 0))
            def _():
                down(r, c).wait_send()

            @pl.when((r != z) & (r != q))
            def _():
                to_owner(r, c).wait_send()

        out_copy(c).wait()


def body(sizes, slab, occupied):
    nr, na, nc, chunks, rows, depth, occ = sizes
    planes, width = na * nc, depth // nc * occ
    block = chunks * rows
    any_space = pl.BlockSpec(memory_space=pl.ANY)
    dma = pltpu.SemaphoreType.DMA
    bf16 = jnp.bfloat16
    return pl.pallas_call(
        functools.partial(kernel, sizes),
        out_shape=jax.ShapeDtypeStruct((block, block), jnp.float32),
        in_specs=[pl.BlockSpec(memory_space=pltpu.MemorySpace.HBM)] * 2,
        out_specs=any_space,
        scratch_shapes=[
            pltpu.VMEM(occupied.shape, bf16),
            pltpu.VMEM((chunks, depth, rows, slab.shape[2]), bf16),
            pltpu.VMEM((chunks, rows, width), jnp.float32),
            pltpu.VMEM((chunks, rows, width), bf16),
            pltpu.VMEM((chunks, rows, width), bf16),
            pltpu.VMEM((nr, chunks, rows, width), bf16),
            pltpu.VMEM((planes, chunks, rows, width), bf16),
            pltpu.VMEM((planes, chunks, rows, width), bf16),
            pltpu.VMEM((chunks, rows, block), jnp.float32),
            dma((chunks,)), dma((chunks,)), dma((chunks,)),
            dma((nr, chunks)), dma((nr, chunks)), dma((nr, chunks)),
            dma((nr, chunks)), dma((planes, chunks)),
            dma((na - 1, chunks)), dma((chunks,)), dma((na - 1, chunks)), dma((planes, chunks)),
            dma((chunks,)), dma,
        ],
        compiler_params=pltpu.CompilerParams(
            collective_id=0, has_side_effects=True, vmem_limit_bytes=48 * 2**20),
    )(slab, occupied)


def solution(mesh):
    nr, na, nc = mesh.shape["row"], mesh.shape["aux"], mesh.shape["col"]
    if nc != 2 or na * nc != nr:
        raise ValueError("unsupported mesh")
    ng = mesh.shape["grp"]

    def run(aux_slab, occupied):
        depth = aux_slab.shape[0] // (ng * na)
        block = aux_slab.shape[1] // nr
        rows = min(128, block)
        sizes = (nr, na, nc, block // rows, rows, depth, occupied.shape[1] // ng)
        in_specs = (P(("grp", "aux"), "row", "col"), P("col", "grp"))
        out_specs = P(("grp", "aux", "col"), "row")
        return jax.shard_map(
            functools.partial(body, sizes), mesh=mesh, in_specs=in_specs, out_specs=out_specs, check_vma=False,
        )(aux_slab, occupied)

    return run
```
